32 devices in a mesh: rep: 2 (over x), exp: 2 (over core), tp: 8 (over z, y).
Axes of the slice: x: 2, y: 2, z: 4, core: 2. Of those that a mesh axis runs over, the one named last changes fastest.
Arguments:
- tokens: bfloat16 [128, 4096], P(('rep', 'exp', 'tp')), parts along dimension 0, may hold values from -6 to 6
- expert_ids: int32 [128, 2], P(('rep', 'exp', 'tp')), parts along dimension 0, may hold values from 0 to 3, all different within a row; in each aligned block of 4 rows (0 to 3, 4 to 7, ...) at most 4 rows name the same one
- gate_ints: int32 [128, 2], P(('rep', 'exp', 'tp')), parts along dimension 0, may hold values from 16 to 240, as said below
- gate_weight: bfloat16 [4, 4096, 14336], P('exp', None, 'tp'), may hold values from -0.09375 to 0.09375
- up_weight: bfloat16 [4, 4096, 14336], P('exp', None, 'tp'), may hold values from -0.09375 to 0.09375
- down_weight: bfloat16 [4, 14336, 4096], P('exp', 'tp'), may hold values from -0.046875 to 0.046875
Outputs:
- mixed: bfloat16 [128, 4096], P(('rep', 'exp', 'tp')), parts along dimension 0
The draws below stay inside these ranges and needn't reach their ends.
There are 2 independent parts, one for each index of `rep`. The reference program is written for one: setup_inputs(seed, part) draws one part's arguments, and reference() takes and returns one part's arrays. A program takes and returns all parts, laid end to end along the dimension named above; an argument that names none is the same for every part. Nothing has to cross between parts.
Inputs may be any that keep to these rules, and one draw needn't show every extreme that they name: `expert_ids`: each row names two different experts. Among the 4 rows of one device an expert is named at most 4 times, and exactly that often on some device. `gate_ints`: the two entries of a row sum to 256.
All inputs are finite; a program needn't handle non-finite values.
Results may differ from the reference program's by a relative error of at most 0.0049.
Values may be sent and summed in bfloat16 or wider, within the bound.
No kernel may reach another device: no remote copies, remote signals or barrier semaphores. Data moves between devices by JAX's collectives and lax.ppermute only.
A program may use at most 128 MiB of HBM per device.

```python
import math
import jax
import jax.numpy as jnp
import numpy as np
from jax import lax

D = 4096
FF = 14336
TOK_DEV = 4
EXPERTS = 4
TOKENS = 64


def draw_gate_ints(key, part):
    first = jax.random.randint(key, (TOKENS,), 16, 241)
    first = first.at[0].set(16)
    return jnp.stack([first, 256 - first], axis=1).astype(jnp.int32)


def block_scale(stream_key, shape, pieces, smallest, largest):
    gain = 1.0
    for axis_at, blocks in pieces:
        steps = jax.random.uniform(jax.random.fold_in(jax.random.fold_in(stream_key, 6), axis_at), (blocks,), jnp.float32, smallest / len(pieces), largest / len(pieces))
        gain = gain * jnp.repeat(jnp.exp(steps), shape[axis_at] // blocks).reshape((-1,) + (1,) * (len(shape) - 1 - axis_at))
    return gain


def assign_block(key, own, number, rows, amount, top, bound, slope):
    sequence = jax.random.permutation(key, amount)
    crowded, usual = load_shares(amount, rows * top, bound, slope, True), load_shares(amount, rows * top, bound, slope, False)
    places = jnp.arange(amount)

    def named(tallies, turn):
        used = int((tallies > 0).sum())
        fixed = max(1, used // 4)
        passed = fixed + (places - fixed + turn * (used - fixed)) % max(1, amount - fixed)
        return jnp.zeros((amount,), jnp.int32).at[sequence[jnp.where(places < fixed, places, passed)]].set(jnp.asarray(tallies, jnp.int32))

    tallies = jnp.where(number % 4 == 0, named(crowded, number // 4), named(usual, number - number // 4 - 1))
    mixed = jax.random.permutation(jax.random.fold_in(own, 3), amount)
    giver, sink = mixed[0:amount // 2 * 2:2], mixed[1:amount // 2 * 2:2]
    slack = jnp.minimum(tallies[giver] - 1, bound - tallies[sink]) // 2
    slack = jnp.where((giver == sequence[0]) | (sink == sequence[0]) | (tallies[sink] == 0), 0, jnp.maximum(slack, 0))
    passed = jax.random.randint(jax.random.fold_in(own, 4), (amount // 2,), 0, 1 << 20) % (slack + 1)
    tallies = tallies.at[giver].add(-passed).at[sink].add(passed)
    items = jnp.searchsorted(jnp.cumsum(tallies), jnp.arange(rows * top), side="right").astype(jnp.int32)
    table = items.reshape(top, rows).T
    table = table[jax.random.permutation(jax.random.fold_in(own, 1), rows)]
    turn = jax.random.randint(jax.random.fold_in(own, 2), (rows, 1), 0, top)
    return jnp.take_along_axis(table, (jnp.arange(top)[None, :] + turn) % top, axis=1)


def load_shares(amount, total, bound, lean, full):
    loads = [(1 << 20) // math.isqrt(grade ** lean) + 1 for grade in range(1, amount + 1)]
    largest = bound if full else min(bound, max(-(-total // amount), total * loads[0] // sum(loads)))
    least = 1 if total - largest >= amount - 1 else 0
    given, spare = [largest] + [least] * (amount - 1), total - largest - least * (amount - 1)
    while spare > 0:
        candidates = [i for i in range(1, amount) if given[i] < largest] or [i for i in range(1, amount) if given[i] < bound]
        whole, left = sum([loads[i] for i in candidates]), spare
        for i in candidates:
            more = min(bound - given[i], max(1, left * loads[i] // whole), spare)
            given[i] = given[i] + more
            spare = spare - more
    return np.array(given)


def gaussian(key, extent, width, bound, pieces=(), kind=jnp.bfloat16):
    loudness = block_scale(key, extent, pieces, -0.22, 0.18) if pieces else 1.0
    drawn = jax.random.normal(key, extent, jnp.float32) * width * loudness
    return jnp.minimum(jnp.maximum(drawn, -bound), bound).astype(kind)


def setup_inputs(seed: int = 0, part: int = 0) -> dict:
    seeds = jax.random.split(jax.random.key(seed), 7)
    part_keys = jax.random.split(jax.random.fold_in(seeds[6], part), 7)
    tokens = gaussian(part_keys[0], (TOKENS, D), 1.0, 6.0, ((0, 16),))
    expert_ids_keys = jax.random.split(jax.random.fold_in(part_keys[1], 1), TOKENS // TOK_DEV)
    expert_ids_turns = jax.random.permutation(jax.random.fold_in(part_keys[1], 3), TOKENS // TOK_DEV)
    expert_ids = jax.vmap(lambda own, number: assign_block(jax.random.fold_in(part_keys[1], 2), own, number, TOK_DEV, EXPERTS, 2, TOK_DEV, 1))(expert_ids_keys, expert_ids_turns).reshape((TOKENS, 2))
    gate_ints = draw_gate_ints(jax.random.fold_in(jax.random.fold_in(seeds[6], part), 71), part)
    gate_weight = gaussian(seeds[3], (EXPERTS, D, FF), D ** -0.5, 0.09375, ((0, 2), (2, 8)))
    up_weight = gaussian(seeds[4], (EXPERTS, D, FF), D ** -0.5, 0.09375, ((0, 2), (2, 8)))
    down_weight = gaussian(seeds[5], (EXPERTS, FF, D), FF ** -0.5, 0.046875, ((0, 2), (1, 8)))
    return dict(tokens=tokens, expert_ids=expert_ids, gate_ints=gate_ints, gate_weight=gate_weight, up_weight=up_weight, down_weight=down_weight)


def reference(tokens, expert_ids, gate_ints, gate_weight, up_weight, down_weight):
    inputs = tokens.astype(jnp.float32)
    gates = gate_ints.astype(jnp.float32) / 256.0

    def accumulate(index, total):
        w_gate = gate_weight[index].astype(jnp.float32)
        w_up = up_weight[index].astype(jnp.float32)
        w_down = down_weight[index].astype(jnp.float32)
        gate = jnp.dot(inputs, w_gate, preferred_element_type=jnp.float32)
        upper = jnp.dot(inputs, w_up, preferred_element_type=jnp.float32)
        hidden = (jax.nn.silu(gate) * upper).astype(jnp.bfloat16)
        output = jnp.dot(hidden.astype(jnp.float32), w_down, preferred_element_type=jnp.float32)
        weight = jnp.sum(jnp.where(expert_ids == index, gates, 0.0), axis=1)
        return total + weight[:, None] * output

    start = jnp.zeros((TOKENS, D), jnp.float32)
    total = lax.fori_loop(0, EXPERTS, accumulate, start)
    return total.astype(jnp.bfloat16)
```

```python
import functools

import jax
import jax.numpy as jnp
from jax import lax
from jax.experimental import pallas as pl
from jax.experimental.pallas import tpu as pltpu
from jax.sharding import PartitionSpec as P

AXES = ("rep", "exp", "tp")
LANES = 128


def partner(mesh_shape, rep_xor, exp_xor, tp_xor):
    reps, exps, tps = mesh_shape
    pairs = []
    for r in range(reps):
        for e in range(exps):
            for t in range(tps):
                here = (r * exps + e) * tps + t
                there = ((r ^ rep_xor) * exps + (e ^ exp_xor)) * tps + (t ^ tp_xor)
                pairs.append((here, there))
    return pairs


def exchange_rounds(mesh_shape):
    reps, _, tps = mesh_shape
    bits = [(0, 1 << b) for b in reversed(range(tps.bit_length() - 1))]
    bits += [(1 << b, 0) for b in range(reps.bit_length() - 1)]
    rounds = []
    for first in range(0, len(bits), 2):
        group = bits[first : first + 2]
        offsets = list(group)
        if len(group) == 2:
            offsets.append((group[0][0] ^ group[1][0], group[0][1] ^ group[1][1]))
        rounds.append(offsets)
    return rounds


def expert_kernel(
    width, experts_here, steps_in, steps_out, near, far, gate_w, up_w, down_w,
    keep, send, gate_v, up_v, down_v, gate_acc, up_acc, out_acc, sems,
):
    half = near.shape[0]
    rep = lax.axis_index("rep")
    first_local = rep * experts_here
    first_global = lax.axis_index("exp") * gate_w.shape[0] + first_local
    rows_in, rows_out = width // steps_in, gate_v.shape[1] // steps_out
    lane = lax.broadcasted_iota(jnp.int32, (half, LANES), 1)

    def in_copies(at, k):
        rows = pl.ds(k * rows_in, rows_in)
        return (
            pltpu.make_async_copy(gate_w.at[first_local + at, rows], gate_v.at[rows], sems.at[2 * k]),
            pltpu.make_async_copy(up_w.at[first_local + at, rows], up_v.at[rows], sems.at[2 * k + 1]),
        )

    def out_copy(at, k):
        rows = pl.ds(k * rows_out, rows_out)
        return pltpu.make_async_copy(
            down_w.at[first_local + at, rows], down_v.at[rows], sems.at[2 * steps_in + k]
        )

    for at in range(experts_here):
        ins = [in_copies(at, k) for k in range(steps_in)]
        outs = [out_copy(at, k) for k in range(steps_out)]
        for gate_copy, up_copy in ins:
            gate_copy.start()
            up_copy.start()
        for copy in outs:
            copy.start()
        for k, (gate_copy, up_copy) in enumerate(ins):
            cols = slice(k * rows_in, (k + 1) * rows_in)
            x = jnp.concatenate([near[:, cols], far[:, cols]], axis=0)
            gate_copy.wait()
            gate = jnp.dot(x, gate_v[cols, :], preferred_element_type=jnp.float32)
            gate_acc[...] = gate if k == 0 else gate_acc[...] + gate
            up_copy.wait()
            upper = jnp.dot(x, up_v[cols, :], preferred_element_type=jnp.float32)
            up_acc[...] = upper if k == 0 else up_acc[...] + upper
        gate = gate_acc[...]
        hidden = (gate / (1.0 + jnp.exp(-gate)) * up_acc[...]).astype(jnp.bfloat16)
        for k, copy in enumerate(outs):
            cols = slice(k * rows_out, (k + 1) * rows_out)
            copy.wait()
            term = jnp.dot(hidden[:, cols], down_v[cols, :], preferred_element_type=jnp.float32)
            out_acc[...] = term if k == 0 else out_acc[...] + term
        chosen = lane == first_global + at
        for rows, tokens, out in ((slice(0, half), near, keep), (slice(half, 2 * half), far, send)):
            tail = tokens[:, width:].astype(jnp.float32)
            weight = jnp.sum(jnp.where(chosen, tail, 0.0), axis=1, keepdims=True)
            scaled = weight * out_acc[rows, :]
            out[...] = (scaled if at == 0 else out[...] + scaled).astype(out.dtype)


def run_experts(near, far, gate_w, up_w, down_w, experts_here):
    half = near.shape[0]
    _, width, hidden = gate_w.shape
    steps_in = 8
    steps_out = hidden // 256 if hidden % 256 == 0 else 1
    any_spec = pl.BlockSpec(memory_space=pl.ANY)
    vmem_spec = pl.BlockSpec(memory_space=pltpu.VMEM)
    send_type = jnp.bfloat16 if experts_here == 1 else jnp.float32
    return pl.pallas_call(
        functools.partial(expert_kernel, width, experts_here, steps_in, steps_out),
        out_shape=(
            jax.ShapeDtypeStruct((half, width), jnp.float32),
            jax.ShapeDtypeStruct((half, width), send_type),
        ),
        in_specs=[vmem_spec, vmem_spec, any_spec, any_spec, any_spec],
        out_specs=(vmem_spec, vmem_spec),
        scratch_shapes=[
            pltpu.VMEM((width, hidden), jnp.bfloat16),
            pltpu.VMEM((width, hidden), jnp.bfloat16),
            pltpu.VMEM((hidden, width), jnp.bfloat16),
            pltpu.VMEM((2 * half, hidden), jnp.float32),
            pltpu.VMEM((2 * half, hidden), jnp.float32),
            pltpu.VMEM((2 * half, width), jnp.float32),
            pltpu.SemaphoreType.DMA((2 * steps_in + steps_out,)),
        ],
        compiler_params=pltpu.CompilerParams(vmem_limit_bytes=56 * 2**20),
    )(near, far, gate_w, up_w, down_w)


def body(mesh_shape, tokens, expert_ids, gate_ints, gate_weight, up_weight, down_weight):
    rows, width = tokens.shape
    experts_here = gate_weight.shape[0] // mesh_shape[0]

    def swap(x, rep_xor, exp_xor, tp_xor):
        return lax.ppermute(x, AXES, partner(mesh_shape, rep_xor, exp_xor, tp_xor))

    lanes = jnp.arange(LANES, dtype=jnp.int32)
    gates = gate_ints.astype(jnp.float32) / 256.0
    weights = jnp.sum(
        jnp.where(expert_ids[:, :, None] == lanes[None, None, :], gates[:, :, None], 0.0), axis=1
    )
    gathered = jnp.concatenate([tokens, weights.astype(jnp.bfloat16)], axis=1)
    rounds = exchange_rounds(mesh_shape)
    for offsets in rounds:
        gathered = jnp.concatenate(
            [gathered] + [swap(gathered, r, 0, t) for r, t in offsets], axis=0
        )
    far = swap(gathered, 0, 1, 0)
    keep, send = run_experts(gathered, far, gate_weight, up_weight, down_weight, experts_here)
    total = keep + swap(send, 0, 1, 0).astype(jnp.float32)
    for offsets in reversed(rounds):
        part = total.shape[0] // (len(offsets) + 1)
        pieces = [total[i * part : (i + 1) * part] for i in range(len(offsets) + 1)]
        total = pieces[0]
        for piece, (r, t) in zip(pieces[1:], offsets):
            total = total + swap(piece.astype(jnp.bfloat16), r, 0, t).astype(jnp.float32)
    return total.astype(jnp.bfloat16)


def solution(mesh):
    mesh_shape = tuple(mesh.shape[a] for a in AXES)
    return jax.shard_map(
        functools.partial(body, mesh_shape),
        mesh=mesh,
        in_specs=(
            P(AXES, None),
            P(AXES, None),
            P(AXES, None),
            P("exp", None, "tp"),
            P("exp", None, "tp"),
            P("exp", "tp", None),
        ),
        out_specs=P(AXES, None),
        check_vma=False,
    )
```

```python
import functools

import jax
import jax.numpy as jnp
from jax import lax
from jax.experimental import pallas as pl
from jax.experimental.pallas import tpu as pltpu
from jax.sharding import PartitionSpec as P

AXES = ("rep", "exp", "tp")
LANES = 128
MIB = 2**20
EARLY_EIGHTHS = (2, 3, 1)
HBM = pl.BlockSpec(memory_space=pltpu.HBM)
VMEM = pl.BlockSpec(memory_space=pltpu.VMEM)
SMEM = pl.BlockSpec(memory_space=pltpu.SMEM)
ANY = pl.BlockSpec(memory_space=pl.ANY)


def partner(mesh_shape, rep_xor, exp_xor, tp_xor):
    reps, exps, tps = mesh_shape
    pairs = []
    for r in range(reps):
        for e in range(exps):
            for t in range(tps):
                here = (r * exps + e) * tps + t
                there = ((r ^ rep_xor) * exps + (e ^ exp_xor)) * tps + (t ^ tp_xor)
                pairs.append((here, there))
    return pairs


def exchange_rounds(mesh_shape):
    reps, _, tps = mesh_shape
    bits = [(0, 1 << b) for b in reversed(range(tps.bit_length() - 1))]
    bits += [(1 << b, 0) for b in range(reps.bit_length() - 1)]
    rounds = []
    for first in range(0, len(bits), 2):
        group = bits[first : first + 2]
        offsets = list(group)
        if len(group) == 2:
            offsets.append((group[0][0] ^ group[1][0], group[0][1] ^ group[1][1]))
        rounds.append(offsets)
    return rounds


def pack_kernel(ids, gates, tokens, packed):
    rows, width = tokens.shape
    packed[:, :width] = tokens[...]
    row = lax.broadcasted_iota(jnp.int32, (rows, LANES), 0)
    lane = lax.broadcasted_iota(jnp.int32, (rows, LANES), 1)
    weights = jnp.zeros((rows, LANES), jnp.float32)
    for t in range(rows):
        for k in range(ids.shape[0]):
            gate = gates[k, t].astype(jnp.float32) / 256.0
            weights += jnp.where((row == t) & (lane == ids[k, t]), gate, 0.0)
    packed[:, width:] = weights.astype(packed.dtype)


def pack(tokens, ids, gates):
    rows, width = tokens.shape
    return pl.pallas_call(
        pack_kernel,
        out_shape=jax.ShapeDtypeStruct((rows, width + LANES), tokens.dtype),
        in_specs=[SMEM, SMEM, VMEM],
        out_specs=VMEM,
        compiler_params=pltpu.CompilerParams(vmem_limit_bytes=2 * MIB),
    )(*(pltpu.with_memory_space_constraint(x, pltpu.HBM) for x in (ids.T, gates.T, tokens)))


def early_kernel(first, gate_w, up_w, after, gate_v, up_v, sems):
    del after
    rep = lax.axis_index("rep")
    rows = pl.ds(first, gate_v.shape[0])
    copies = [
        pltpu.make_async_copy(gate_w.at[rep, rows], gate_v, sems.at[0]),
        pltpu.make_async_copy(up_w.at[rep, rows], up_v, sems.at[1]),
    ]
    for copy in copies:
        copy.start()
    for copy in copies:
        copy.wait()


def load_early(gate_w, up_w, after, first, rows):
    hidden = gate_w.shape[2]
    size = rows * hidden * gate_w.dtype.itemsize
    return pl.pallas_call(
        functools.partial(early_kernel, first),
        out_shape=(pltpu.VMEM((rows, hidden), gate_w.dtype),) * 2,
        in_specs=[HBM, HBM, ANY],
        out_specs=(VMEM, VMEM),
        scratch_shapes=[pltpu.SemaphoreType.DMA((2,))],
        compiler_params=pltpu.CompilerParams(vmem_limit_bytes=MIB),
        cost_estimate=pl.CostEstimate(flops=0, bytes_accessed=4 * size, transcendentals=0),
    )(gate_w, up_w, after)


def expert_kernel(early, late_steps, down_steps, *refs):
    near, far, gate_w, up_w, down_w = refs[:5]
    loaded = refs[5 : 5 + 2 * early]
    keep, send, gate_v, up_v, down_v, gate_acc, up_acc, out_acc, sems = refs[5 + 2 * early :]
    half = near.shape[0]
    width = keep.shape[1]
    rep = lax.axis_index("rep")
    expert = lax.axis_index("exp") * gate_w.shape[0] + rep
    late_rows, hidden_width = gate_v.shape
    late_first = width - late_rows
    step_rows, down_rows = late_rows // late_steps, hidden_width // down_steps

    late, down = [], []
    for k in range(late_steps):
        there, here = pl.ds(late_first + k * step_rows, step_rows), pl.ds(k * step_rows, step_rows)
        late.append(
            (
                pltpu.make_async_copy(gate_w.at[rep, there], gate_v.at[here], sems.at[2 * k]),
                pltpu.make_async_copy(up_w.at[rep, there], up_v.at[here], sems.at[2 * k + 1]),
            )
        )
    for k in range(down_steps):
        rows = pl.ds(k * down_rows, down_rows)
        down.append(
            pltpu.make_async_copy(down_w.at[rep, rows], down_v.at[rows], sems.at[2 * late_steps + k])
        )
    for pair in late:
        for copy in pair:
            copy.start()
    for copy in down:
        copy.start()

    def tokens(first, rows):
        cols = slice(first, first + rows)
        return jnp.concatenate([near[:, cols], far[:, cols]], axis=0)

    first = 0
    for k in range(early):
        gate_p, up_p = loaded[2 * k], loaded[2 * k + 1]
        x = tokens(first, gate_p.shape[0])
        gate = jnp.dot(x, gate_p[...], preferred_element_type=jnp.float32)
        gate_acc[...] = gate if k == 0 else gate_acc[...] + gate
        upper = jnp.dot(x, up_p[...], preferred_element_type=jnp.float32)
        up_acc[...] = upper if k == 0 else up_acc[...] + upper
        first += gate_p.shape[0]
    for k, (gate_copy, up_copy) in enumerate(late):
        here = slice(k * step_rows, (k + 1) * step_rows)
        x = tokens(first, step_rows)
        gate_copy.wait()
        gate_acc[...] += jnp.dot(x, gate_v[here, :], preferred_element_type=jnp.float32)
        up_copy.wait()
        up_acc[...] += jnp.dot(x, up_v[here, :], preferred_element_type=jnp.float32)
        first += step_rows
    gate = gate_acc[...]
    hidden = (gate / (1.0 + jnp.exp(-gate)) * up_acc[...]).astype(jnp.bfloat16)
    for k, copy in enumerate(down):
        cols = slice(k * down_rows, (k + 1) * down_rows)
        copy.wait()
        term = jnp.dot(hidden[:, cols], down_v[cols, :], preferred_element_type=jnp.float32)
        out_acc[...] = term if k == 0 else out_acc[...] + term
    chosen = lax.broadcasted_iota(jnp.int32, (half, LANES), 1) == expert
    for rows, piece, out in ((slice(half, 2 * half), far, send), (slice(0, half), near, keep)):
        tail = piece[:, width:].astype(jnp.float32)
        weight = jnp.sum(jnp.where(chosen, tail, 0.0), axis=1, keepdims=True)
        out[...] = (weight * out_acc[rows, :]).astype(out.dtype)


def run_experts(near, far, loaded, gate_w, up_w, down_w):
    half = near.shape[0]
    _, width, hidden = gate_w.shape
    padded = -(-hidden // LANES) * LANES
    late_rows = width - sum(gate_p.shape[0] for gate_p, _ in loaded)
    late_steps = 2
    down_steps = hidden // 256 if hidden % 256 == 0 else 1
    scratch = 4 * late_rows * padded + 2 * hidden * width + 8 * half * (2 * padded + width)
    return pl.pallas_call(
        functools.partial(expert_kernel, len(loaded), late_steps, down_steps),
        out_shape=(
            jax.ShapeDtypeStruct((half, width), jnp.float32),
            jax.ShapeDtypeStruct((half, width), jnp.bfloat16),
        ),
        in_specs=[VMEM, VMEM, HBM, HBM, HBM] + [VMEM] * (2 * len(loaded)),
        out_specs=(VMEM, VMEM),
        scratch_shapes=[
            pltpu.VMEM((late_rows, hidden), jnp.bfloat16),
            pltpu.VMEM((late_rows, hidden), jnp.bfloat16),
            pltpu.VMEM((hidden, width), jnp.bfloat16),
            pltpu.VMEM((2 * half, hidden), jnp.float32),
            pltpu.VMEM((2 * half, hidden), jnp.float32),
            pltpu.VMEM((2 * half, width), jnp.float32),
            pltpu.SemaphoreType.DMA((2 * late_steps + down_steps,)),
        ],
        compiler_params=pltpu.CompilerParams(vmem_limit_bytes=scratch + 4 * MIB),
    )(near, far, gate_w, up_w, down_w, *(ref for pair in loaded for ref in pair))


def body(mesh_shape, tokens, expert_ids, gate_ints, gate_weight, up_weight, down_weight):
    width = tokens.shape[1]
    assert gate_weight.shape[0] == mesh_shape[0]
    gate_weight, up_weight, down_weight = (
        pltpu.with_memory_space_constraint(w, pltpu.HBM)
        for w in (gate_weight, up_weight, down_weight)
    )

    def swap(x, rep_xor, exp_xor, tp_xor):
        return lax.ppermute(x, AXES, partner(mesh_shape, rep_xor, exp_xor, tp_xor))

    gathered = pack(tokens, expert_ids, gate_ints)
    rounds = exchange_rounds(mesh_shape)
    shares = [e * width // 8 for e in EARLY_EIGHTHS]
    loaded, first = [], 0

    def load(rows):
        nonlocal first
        loaded.append(load_early(gate_weight, up_weight, gathered, first, rows))
        first += rows

    for at, offsets in enumerate(rounds):
        if at < len(shares) - 1:
            load(shares[at])
        gathered = jnp.concatenate(
            [gathered] + [swap(gathered, r, 0, t) for r, t in offsets], axis=0
        )
        if at < len(shares) - 1:
            gathered, loaded[-1] = lax.optimization_barrier((gathered, loaded[-1]))
    load(shares[-1])
    far = swap(gathered, 0, 1, 0)
    keep, send = run_experts(gathered, far, loaded, gate_weight, up_weight, down_weight)
    total = keep + swap(send, 0, 1, 0).astype(jnp.float32)
    for offsets in reversed(rounds):
        part = total.shape[0] // (len(offsets) + 1)
        pieces = [total[i * part : (i + 1) * part] for i in range(len(offsets) + 1)]
        total = pieces[0]
        for piece, (r, t) in zip(pieces[1:], offsets):
            total = total + swap(piece.astype(jnp.bfloat16), r, 0, t).astype(jnp.float32)
    return total.astype(jnp.bfloat16)


def solution(mesh):
    mesh_shape = tuple(mesh.shape[a] for a in AXES)
    return jax.shard_map(
        functools.partial(body, mesh_shape),
        mesh=mesh,
        in_specs=(
            P(AXES, None),
            P(AXES, None),
            P(AXES, None),
            P("exp", None, "tp"),
            P("exp", None, "tp"),
            P("exp", "tp", None),
        ),
        out_specs=P(AXES, None),
        check_vma=False,
    )
```

```python
import functools

import jax
import jax.numpy as jnp
from jax import lax
from jax.experimental import pallas as pl
from jax.experimental.pallas import tpu as pltpu
from jax.sharding import PartitionSpec as P

AXES = ("rep", "exp", "tp")
LANES = 128
MIB = 2**20
EARLY_SHARES = (5, 7, 2)
HBM = pl.BlockSpec(memory_space=pltpu.HBM)
VMEM = pl.BlockSpec(memory_space=pltpu.VMEM)
SMEM = pl.BlockSpec(memory_space=pltpu.SMEM)
ANY = pl.BlockSpec(memory_space=pl.ANY)


def partner(mesh_shape, rep_xor, exp_xor, tp_xor):
    reps, exps, tps = mesh_shape
    pairs = []
    for r in range(reps):
        for e in range(exps):
            for t in range(tps):
                here = (r * exps + e) * tps + t
                there = ((r ^ rep_xor) * exps + (e ^ exp_xor)) * tps + (t ^ tp_xor)
                pairs.append((here, there))
    return pairs


def exchange_rounds(mesh_shape):
    reps, _, tps = mesh_shape
    bits = [(0, 1 << b) for b in reversed(range(tps.bit_length() - 1))]
    bits += [(1 << b, 0) for b in range(reps.bit_length() - 1)]
    rounds = []
    for first in range(0, len(bits), 2):
        group = bits[first : first + 2]
        offsets = list(group)
        if len(group) == 2:
            offsets.append((group[0][0] ^ group[1][0], group[0][1] ^ group[1][1]))
        rounds.append(offsets)
    return rounds


def pack_kernel(ids, gates, tokens, packed):
    rows, width = tokens.shape
    packed[:, :width] = tokens[...]
    row = lax.broadcasted_iota(jnp.int32, (rows, LANES), 0)
    lane = lax.broadcasted_iota(jnp.int32, (rows, LANES), 1)
    weights = jnp.zeros((rows, LANES), jnp.float32)
    for t in range(rows):
        for k in range(ids.shape[0]):
            gate = gates[k, t].astype(jnp.float32) / 256.0
            weights += jnp.where((row == t) & (lane == ids[k, t]), gate, 0.0)
    packed[:, width:] = weights.astype(packed.dtype)


def pack(tokens, ids, gates):
    rows, width = tokens.shape
    return pl.pallas_call(
        pack_kernel,
        out_shape=jax.ShapeDtypeStruct((rows, width + LANES), tokens.dtype),
        in_specs=[SMEM, SMEM, VMEM],
        out_specs=VMEM,
        compiler_params=pltpu.CompilerParams(vmem_limit_bytes=2 * MIB),
    )(*(pltpu.with_memory_space_constraint(x, pltpu.HBM) for x in (ids.T, gates.T, tokens)))


def early_kernel(first, gate_w, up_w, after, gate_v, up_v, sems):
    del after
    rep = lax.axis_index("rep")
    rows = pl.ds(first, gate_v.shape[0])
    copies = [
        pltpu.make_async_copy(gate_w.at[rep, rows], gate_v, sems.at[0]),
        pltpu.make_async_copy(up_w.at[rep, rows], up_v, sems.at[1]),
    ]
    for copy in copies:
        copy.start()
    for copy in copies:
        copy.wait()


def load_early(gate_w, up_w, after, first, rows):
    hidden = gate_w.shape[2]
    size = rows * hidden * gate_w.dtype.itemsize
    return pl.pallas_call(
        functools.partial(early_kernel, first),
        out_shape=(pltpu.VMEM((rows, hidden), gate_w.dtype),) * 2,
        in_specs=[HBM, HBM, ANY],
        out_specs=(VMEM, VMEM),
        scratch_shapes=[pltpu.SemaphoreType.DMA((2,))],
        compiler_params=pltpu.CompilerParams(vmem_limit_bytes=MIB),
        cost_estimate=pl.CostEstimate(flops=0, bytes_accessed=4 * size, transcendentals=0),
    )(gate_w, up_w, after)


def expert_kernel(early, late_steps, down_steps, *refs):
    near, far, gate_w, up_w, down_w = refs[:5]
    loaded = refs[5 : 5 + 2 * early]
    keep, send, lead, gate_v, up_v, down_v, gate_acc, up_acc, out_acc, sems = refs[5 + 2 * early :]
    half = near.shape[0]
    width = keep.shape[1]
    rep = lax.axis_index("rep")
    expert = lax.axis_index("exp") * gate_w.shape[0] + rep
    late_rows, hidden_width = gate_v.shape
    late_first = width - late_rows
    step_rows, down_rows = late_rows // late_steps, hidden_width // down_steps

    late, down = [], []
    for k in range(late_steps):
        there, here = pl.ds(late_first + k * step_rows, step_rows), pl.ds(k * step_rows, step_rows)
        late.append(
            (
                pltpu.make_async_copy(gate_w.at[rep, there], gate_v.at[here], sems.at[2 * k]),
                pltpu.make_async_copy(up_w.at[rep, there], up_v.at[here], sems.at[2 * k + 1]),
            )
        )
    for k in range(down_steps):
        rows = pl.ds(k * down_rows, down_rows)
        down.append(
            pltpu.make_async_copy(down_w.at[rep, rows], down_v.at[rows], sems.at[2 * late_steps + k])
        )
    for pair in late:
        for copy in pair:
            copy.start()
    for copy in down:
        copy.start()
    lead_cols = pl.ds(0, lead.shape[1])
    last = 2 * late_steps + down_steps
    leads = [
        pltpu.make_async_copy(near.at[:, lead_cols], lead.at[pl.ds(0, half)], sems.at[last]),
        pltpu.make_async_copy(far.at[:, lead_cols], lead.at[pl.ds(half, half)], sems.at[last + 1]),
    ]
    for copy in leads:
        copy.start()
    for copy in leads:
        copy.wait()

    def tokens(first, rows):
        if first == 0:
            return lead[...]
        cols = slice(first, first + rows)
        return jnp.concatenate([near[:, cols], far[:, cols]], axis=0)

    first = 0
    for k in range(early):
        gate_p, up_p = loaded[2 * k], loaded[2 * k + 1]
        x = tokens(first, gate_p.shape[0])
        gate = jnp.dot(x, gate_p[...], preferred_element_type=jnp.float32)
        gate_acc[...] = gate if k == 0 else gate_acc[...] + gate
        upper = jnp.dot(x, up_p[...], preferred_element_type=jnp.float32)
        up_acc[...] = upper if k == 0 else up_acc[...] + upper
        first += gate_p.shape[0]
    for k, (gate_copy, up_copy) in enumerate(late):
        here = slice(k * step_rows, (k + 1) * step_rows)
        x = tokens(first, step_rows)
        gate_copy.wait()
        gate_acc[...] += jnp.dot(x, gate_v[here, :], preferred_element_type=jnp.float32)
        up_copy.wait()
        up_acc[...] += jnp.dot(x, up_v[here, :], preferred_element_type=jnp.float32)
        first += step_rows
    gate = gate_acc[...]
    hidden = (gate / (1.0 + jnp.exp(-gate)) * up_acc[...]).astype(jnp.bfloat16)
    for k, copy in enumerate(down):
        cols = slice(k * down_rows, (k + 1) * down_rows)
        copy.wait()
        term = jnp.dot(hidden[:, cols], down_v[cols, :], preferred_element_type=jnp.float32)
        out_acc[...] = term if k == 0 else out_acc[...] + term
    chosen = lax.broadcasted_iota(jnp.int32, (half, LANES), 1) == expert
    for rows, piece, out in ((slice(half, 2 * half), far, send), (slice(0, half), near, keep)):
        tail = piece[:, width:].astype(jnp.float32)
        weight = jnp.sum(jnp.where(chosen, tail, 0.0), axis=1, keepdims=True)
        out[...] = (weight * out_acc[rows, :]).astype(out.dtype)


def run_experts(near, far, loaded, gate_w, up_w, down_w):
    half = near.shape[0]
    _, width, hidden = gate_w.shape
    padded = -(-hidden // LANES) * LANES
    late_rows = width - sum(gate_p.shape[0] for gate_p, _ in loaded)
    late_steps = 2
    down_steps = hidden // 256 if hidden % 256 == 0 else 1
    lead_rows = loaded[0][0].shape[0]
    scratch = 4 * half * lead_rows + 4 * late_rows * padded + 2 * hidden * width + 8 * half * (2 * padded + width)
    return pl.pallas_call(
        functools.partial(expert_kernel, len(loaded), late_steps, down_steps),
        out_shape=(
            jax.ShapeDtypeStruct((half, width), jnp.float32),
            jax.ShapeDtypeStruct((half, width), jnp.bfloat16),
        ),
        in_specs=[VMEM, VMEM, HBM, HBM, HBM] + [VMEM] * (2 * len(loaded)),
        out_specs=(VMEM, VMEM),
        scratch_shapes=[
            pltpu.VMEM((2 * half, lead_rows), jnp.bfloat16),
            pltpu.VMEM((late_rows, hidden), jnp.bfloat16),
            pltpu.VMEM((late_rows, hidden), jnp.bfloat16),
            pltpu.VMEM((hidden, width), jnp.bfloat16),
            pltpu.VMEM((2 * half, hidden), jnp.float32),
            pltpu.VMEM((2 * half, hidden), jnp.float32),
            pltpu.VMEM((2 * half, width), jnp.float32),
            pltpu.SemaphoreType.DMA((2 * late_steps + down_steps + 2,)),
        ],
        compiler_params=pltpu.CompilerParams(vmem_limit_bytes=scratch + 4 * MIB),
    )(near, far, gate_w, up_w, down_w, *(ref for pair in loaded for ref in pair))


def body(mesh_shape, tokens, expert_ids, gate_ints, gate_weight, up_weight, down_weight):
    width = tokens.shape[1]
    assert gate_weight.shape[0] == mesh_shape[0]
    gate_weight, up_weight, down_weight = (
        pltpu.with_memory_space_constraint(w, pltpu.HBM)
        for w in (gate_weight, up_weight, down_weight)
    )

    def swap(x, rep_xor, exp_xor, tp_xor):
        return lax.ppermute(x, AXES, partner(mesh_shape, rep_xor, exp_xor, tp_xor))

    gathered = pack(tokens, expert_ids, gate_ints)
    rounds = exchange_rounds(mesh_shape)
    shares = [e * width // 16 for e in EARLY_SHARES]
    loaded, first = [], 0

    def load(rows):
        nonlocal first
        loaded.append(load_early(gate_weight, up_weight, gathered, first, rows))
        first += rows

    for at, offsets in enumerate(rounds):
        if at < len(shares) - 1:
            load(shares[at])
        gathered = jnp.concatenate(
            [gathered] + [swap(gathered, r, 0, t) for r, t in offsets], axis=0
        )
        if at < len(shares) - 1:
            gathered, loaded[-1] = lax.optimization_barrier((gathered, loaded[-1]))
    load(shares[-1])
    far = swap(gathered, 0, 1, 0)
    keep, send = run_experts(gathered, far, loaded, gate_weight, up_weight, down_weight)
    total = keep + swap(send, 0, 1, 0).astype(jnp.float32)
    for offsets in reversed(rounds):
        part = total.shape[0] // (len(offsets) + 1)
        pieces = [total[i * part : (i + 1) * part] for i in range(len(offsets) + 1)]
        total = pieces[0]
        for piece, (r, t) in zip(pieces[1:], offsets):
            total = total + swap(piece.astype(jnp.bfloat16), r, 0, t).astype(jnp.float32)
    return total.astype(jnp.bfloat16)


def solution(mesh):
    mesh_shape = tuple(mesh.shape[a] for a in AXES)
    return jax.shard_map(
        functools.partial(body, mesh_shape),
        mesh=mesh,
        in_specs=(
            P(AXES, None),
            P(AXES, None),
            P(AXES, None),
            P("exp", None, "tp"),
            P("exp", None, "tp"),
            P("exp", "tp", None),
        ),
        out_specs=P(AXES, None),
        check_vma=False,
    )
```

```python
import functools

import jax
import jax.numpy as jnp
from jax import lax
from jax.experimental import pallas as pl
from jax.experimental.pallas import tpu as pltpu
from jax.sharding import PartitionSpec as P

AXES = ("rep", "exp", "tp")
LANES = 128
MIB = 2**20
EARLY_SHARES = (5, 7, 2)
HBM = pl.BlockSpec(memory_space=pltpu.HBM)
VMEM = pl.BlockSpec(memory_space=pltpu.VMEM)
SMEM = pl.BlockSpec(memory_space=pltpu.SMEM)
ANY = pl.BlockSpec(memory_space=pl.ANY)


def partner(mesh_shape, rep_xor, exp_xor, tp_xor):
    reps, exps, tps = mesh_shape
    pairs = []
    for r in range(reps):
        for e in range(exps):
            for t in range(tps):
                here = (r * exps + e) * tps + t
                there = ((r ^ rep_xor) * exps + (e ^ exp_xor)) * tps + (t ^ tp_xor)
                pairs.append((here, there))
    return pairs


def exchange_rounds(mesh_shape):
    reps, _, tps = mesh_shape
    bits = [(0, 1 << b) for b in reversed(range(tps.bit_length() - 1))]
    bits += [(1 << b, 0) for b in range(reps.bit_length() - 1)]
    rounds = []
    for first in range(0, len(bits), 2):
        group = bits[first : first + 2]
        if len(group) == 2:
            group.append((group[0][0] ^ group[1][0], group[0][1] ^ group[1][1]))
            if first + 2 < len(bits):
                group.reverse()
        rounds.append(group)
    return rounds


def pack_kernel(ids, gates, tokens, packed):
    rows, width = tokens.shape
    packed[:, :width] = tokens[...]
    row = lax.broadcasted_iota(jnp.int32, (rows, LANES), 0)
    lane = lax.broadcasted_iota(jnp.int32, (rows, LANES), 1)
    weights = jnp.zeros((rows, LANES), jnp.float32)
    for t in range(rows):
        for k in range(ids.shape[0]):
            gate = gates[k, t].astype(jnp.float32) / 256.0
            weights += jnp.where((row == t) & (lane == ids[k, t]), gate, 0.0)
    packed[:, width:] = weights.astype(packed.dtype)


def pack(tokens, ids, gates):
    rows, width = tokens.shape
    return pl.pallas_call(
        pack_kernel,
        out_shape=jax.ShapeDtypeStruct((rows, width + LANES), tokens.dtype),
        in_specs=[SMEM, SMEM, VMEM],
        out_specs=VMEM,
        compiler_params=pltpu.CompilerParams(vmem_limit_bytes=2 * MIB),
    )(*(pltpu.with_memory_space_constraint(x, pltpu.HBM) for x in (ids.T, gates.T, tokens)))


def early_kernel(first, gate_w, up_w, after, gate_v, up_v, sems):
    del after
    rep = lax.axis_index("rep")
    rows = pl.ds(first, gate_v.shape[0])
    copies = [
        pltpu.make_async_copy(gate_w.at[rep, rows], gate_v, sems.at[0]),
        pltpu.make_async_copy(up_w.at[rep, rows], up_v, sems.at[1]),
    ]
    for copy in copies:
        copy.start()
    for copy in copies:
        copy.wait()


def load_early(gate_w, up_w, after, first, rows):
    hidden = gate_w.shape[2]
    size = rows * hidden * gate_w.dtype.itemsize
    return pl.pallas_call(
        functools.partial(early_kernel, first),
        out_shape=(pltpu.VMEM((rows, hidden), gate_w.dtype),) * 2,
        in_specs=[HBM, HBM, ANY],
        out_specs=(VMEM, VMEM),
        scratch_shapes=[pltpu.SemaphoreType.DMA((2,))],
        compiler_params=pltpu.CompilerParams(vmem_limit_bytes=MIB),
        cost_estimate=pl.CostEstimate(flops=0, bytes_accessed=4 * size, transcendentals=0),
    )(gate_w, up_w, after)


def expert_kernel(early, late_steps, down_steps, *refs):
    near, far, gate_w, up_w, down_w = refs[:5]
    loaded = refs[5 : 5 + 2 * early]
    keep, send, lead, gate_v, up_v, down_v, gate_acc, up_acc, out_acc, sems = refs[5 + 2 * early :]
    half = near.shape[0]
    width = keep.shape[1]
    rep = lax.axis_index("rep")
    expert = lax.axis_index("exp") * gate_w.shape[0] + rep
    late_rows, hidden_width = gate_v.shape
    late_first = width - late_rows
    step_rows, down_rows = late_rows // late_steps, hidden_width // down_steps

    late, down = [], []
    for k in range(late_steps):
        there, here = pl.ds(late_first + k * step_rows, step_rows), pl.ds(k * step_rows, step_rows)
        late.append(
            (
                pltpu.make_async_copy(gate_w.at[rep, there], gate_v.at[here], sems.at[2 * k]),
                pltpu.make_async_copy(up_w.at[rep, there], up_v.at[here], sems.at[2 * k + 1]),
            )
        )
    for k in range(down_steps):
        rows = pl.ds(k * down_rows, down_rows)
        down.append(
            pltpu.make_async_copy(down_w.at[rep, rows], down_v.at[rows], sems.at[2 * late_steps + k])
        )
    for pair in late:
        for copy in pair:
            copy.start()
    for copy in down:
        copy.start()
    lead_cols = pl.ds(0, lead.shape[1])
    last = 2 * late_steps + down_steps
    leads = [
        pltpu.make_async_copy(near.at[:, lead_cols], lead.at[pl.ds(0, half)], sems.at[last]),
        pltpu.make_async_copy(far.at[:, lead_cols], lead.at[pl.ds(half, half)], sems.at[last + 1]),
    ]
    for copy in leads:
        copy.start()
    for copy in leads:
        copy.wait()

    def tokens(first, rows):
        if first == 0:
            return lead[...]
        cols = slice(first, first + rows)
        return jnp.concatenate([near[:, cols], far[:, cols]], axis=0)

    first = 0
    for k in range(early):
        gate_p, up_p = loaded[2 * k], loaded[2 * k + 1]
        x = tokens(first, gate_p.shape[0])
        gate = jnp.dot(x, gate_p[...], preferred_element_type=jnp.float32)
        gate_acc[...] = gate if k == 0 else gate_acc[...] + gate
        upper = jnp.dot(x, up_p[...], preferred_element_type=jnp.float32)
        up_acc[...] = upper if k == 0 else up_acc[...] + upper
        first += gate_p.shape[0]
    for k, (gate_copy, up_copy) in enumerate(late):
        here = slice(k * step_rows, (k + 1) * step_rows)
        x = tokens(first, step_rows)
        gate_copy.wait()
        gate_acc[...] += jnp.dot(x, gate_v[here, :], preferred_element_type=jnp.float32)
        up_copy.wait()
        up_acc[...] += jnp.dot(x, up_v[here, :], preferred_element_type=jnp.float32)
        first += step_rows
    gate = gate_acc[...]
    hidden = (gate / (1.0 + jnp.exp(-gate)) * up_acc[...]).astype(jnp.bfloat16)
    for k, copy in enumerate(down):
        cols = slice(k * down_rows, (k + 1) * down_rows)
        copy.wait()
        term = jnp.dot(hidden[:, cols], down_v[cols, :], preferred_element_type=jnp.float32)
        out_acc[...] = term if k == 0 else out_acc[...] + term
    chosen = lax.broadcasted_iota(jnp.int32, (half, LANES), 1) == expert
    for rows, piece, out in ((slice(half, 2 * half), far, send), (slice(0, half), near, keep)):
        tail = piece[:, width:].astype(jnp.float32)
        weight = jnp.sum(jnp.where(chosen, tail, 0.0), axis=1, keepdims=True)
        out[...] = (weight * out_acc[rows, :]).astype(out.dtype)


def run_experts(near, far, loaded, gate_w, up_w, down_w):
    half = near.shape[0]
    _, width, hidden = gate_w.shape
    padded = -(-hidden // LANES) * LANES
    late_rows = width - sum(gate_p.shape[0] for gate_p, _ in loaded)
    late_steps = 2
    down_steps = hidden // 256 if hidden % 256 == 0 else 1
    lead_rows = loaded[0][0].shape[0]
    scratch = 4 * half * lead_rows + 4 * late_rows * padded + 2 * hidden * width + 8 * half * (2 * padded + width)
    return pl.pallas_call(
        functools.partial(expert_kernel, len(loaded), late_steps, down_steps),
        out_shape=(
            jax.ShapeDtypeStruct((half, width), jnp.float32),
            jax.ShapeDtypeStruct((half, width), jnp.bfloat16),
        ),
        in_specs=[VMEM, VMEM, HBM, HBM, HBM] + [VMEM] * (2 * len(loaded)),
        out_specs=(VMEM, VMEM),
        scratch_shapes=[
            pltpu.VMEM((2 * half, lead_rows), jnp.bfloat16),
            pltpu.VMEM((late_rows, hidden), jnp.bfloat16),
            pltpu.VMEM((late_rows, hidden), jnp.bfloat16),
            pltpu.VMEM((hidden, width), jnp.bfloat16),
            pltpu.VMEM((2 * half, hidden), jnp.float32),
            pltpu.VMEM((2 * half, hidden), jnp.float32),
            pltpu.VMEM((2 * half, width), jnp.float32),
            pltpu.SemaphoreType.DMA((2 * late_steps + down_steps + 2,)),
        ],
        compiler_params=pltpu.CompilerParams(vmem_limit_bytes=scratch + 4 * MIB),
    )(near, far, gate_w, up_w, down_w, *(ref for pair in loaded for ref in pair))


def body(mesh_shape, tokens, expert_ids, gate_ints, gate_weight, up_weight, down_weight):
    width = tokens.shape[1]
    assert gate_weight.shape[0] == mesh_shape[0]
    gate_weight, up_weight, down_weight = (
        pltpu.with_memory_space_constraint(w, pltpu.HBM)
        for w in (gate_weight, up_weight, down_weight)
    )

    def swap(x, rep_xor, exp_xor, tp_xor):
        return lax.ppermute(x, AXES, partner(mesh_shape, rep_xor, exp_xor, tp_xor))

    gathered = pack(tokens, expert_ids, gate_ints)
    rounds = exchange_rounds(mesh_shape)
    shares = [e * width // 16 for e in EARLY_SHARES]
    loaded, first = [], 0

    def load(rows):
        nonlocal first
        loaded.append(load_early(gate_weight, up_weight, gathered, first, rows))
        first += rows

    for at, offsets in enumerate(rounds):
        if at < len(shares) - 1:
            load(shares[at])
        gathered = jnp.concatenate(
            [gathered] + [swap(gathered, r, 0, t) for r, t in offsets], axis=0
        )
        if at < len(shares) - 1:
            gathered, loaded[-1] = lax.optimization_barrier((gathered, loaded[-1]))
    load(shares[-1])
    far = swap(gathered, 0, 1, 0)
    keep, send = run_experts(gathered, far, loaded, gate_weight, up_weight, down_weight)
    total = keep + swap(send, 0, 1, 0).astype(jnp.float32)
    for offsets in reversed(rounds):
        part = total.shape[0] // (len(offsets) + 1)
        pieces = [total[i * part : (i + 1) * part] for i in range(len(offsets) + 1)]
        total = pieces[0]
        moves = list(zip(pieces[1:], offsets))
        for piece, (r, t) in moves if offsets is rounds[-1] else reversed(moves):
            total = total + swap(piece.astype(jnp.bfloat16), r, 0, t).astype(jnp.float32)
    return total.astype(jnp.bfloat16)


def solution(mesh):
    mesh_shape = tuple(mesh.shape[a] for a in AXES)
    return jax.shard_map(
        functools.partial(body, mesh_shape),
        mesh=mesh,
        in_specs=(
            P(AXES, None),
            P(AXES, None),
            P(AXES, None),
            P("exp", None, "tp"),
            P("exp", None, "tp"),
            P("exp", "tp", None),
        ),
        out_specs=P(AXES, None),
        check_vma=False,
    )
```

```python
import functools

import jax
import jax.numpy as jnp
from jax import lax
from jax.experimental import pallas as pl
from jax.experimental.pallas import tpu as pltpu
from jax.sharding import PartitionSpec as P

AXES = ("rep", "exp", "tp")
LANES = 128
MIB = 2**20
EARLY_SHARES = (5, 7, 2)
HBM = pl.BlockSpec(memory_space=pltpu.HBM)
VMEM = pl.BlockSpec(memory_space=pltpu.VMEM)
SMEM = pl.BlockSpec(memory_space=pltpu.SMEM)
ANY = pl.BlockSpec(memory_space=pl.ANY)


def partner(mesh_shape, exp_xor, offsets):
    reps, exps, tps = mesh_shape
    pairs = []
    for r in range(reps):
        for e in range(exps):
            rep_xor, tp_xor = offsets[e % 2]
            for t in range(tps):
                here = (r * exps + e) * tps + t
                there = ((r ^ rep_xor) * exps + (e ^ exp_xor)) * tps + (t ^ tp_xor)
                pairs.append((here, there))
    return pairs


def exchange_rounds(mesh_shape):
    reps, _, tps = mesh_shape
    bits = [(0, 1 << b) for b in reversed(range(tps.bit_length() - 1))]
    bits += [(1 << b, 0) for b in range(reps.bit_length() - 1)]
    rounds = []
    for first in range(0, len(bits), 2):
        group = bits[first : first + 2]
        if len(group) == 2:
            group.append((group[0][0] ^ group[1][0], group[0][1] ^ group[1][1]))
            if first + 2 < len(bits):
                group.reverse()
        other = group
        if len(group) == 3 and first + 2 >= len(bits):
            other = [group[1], group[0], group[2]]
        rounds.append(list(zip(group, other)))
    return rounds


def pack_kernel(ids, gates, tokens, packed):
    rows, width = tokens.shape
    packed[:, :width] = tokens[...]
    row = lax.broadcasted_iota(jnp.int32, (rows, LANES), 0)
    lane = lax.broadcasted_iota(jnp.int32, (rows, LANES), 1)
    weights = jnp.zeros((rows, LANES), jnp.float32)
    for t in range(rows):
        for k in range(ids.shape[0]):
            gate = gates[k, t].astype(jnp.float32) / 256.0
            weights += jnp.where((row == t) & (lane == ids[k, t]), gate, 0.0)
    packed[:, width:] = weights.astype(packed.dtype)


def pack(tokens, ids, gates):
    rows, width = tokens.shape
    return pl.pallas_call(
        pack_kernel,
        out_shape=jax.ShapeDtypeStruct((rows, width + LANES), tokens.dtype),
        in_specs=[SMEM, SMEM, VMEM],
        out_specs=VMEM,
        compiler_params=pltpu.CompilerParams(vmem_limit_bytes=2 * MIB),
    )(*(pltpu.with_memory_space_constraint(x, pltpu.HBM) for x in (ids.T, gates.T, tokens)))


def early_kernel(first, gate_w, up_w, after, gate_v, up_v, sems):
    del after
    rep = lax.axis_index("rep")
    rows = pl.ds(first, gate_v.shape[0])
    copies = [
        pltpu.make_async_copy(gate_w.at[rep, rows], gate_v, sems.at[0]),
        pltpu.make_async_copy(up_w.at[rep, rows], up_v, sems.at[1]),
    ]
    for copy in copies:
        copy.start()
    for copy in copies:
        copy.wait()


def load_early(gate_w, up_w, after, first, rows):
    hidden = gate_w.shape[2]
    size = rows * hidden * gate_w.dtype.itemsize
    return pl.pallas_call(
        functools.partial(early_kernel, first),
        out_shape=(pltpu.VMEM((rows, hidden), gate_w.dtype),) * 2,
        in_specs=[HBM, HBM, ANY],
        out_specs=(VMEM, VMEM),
        scratch_shapes=[pltpu.SemaphoreType.DMA((2,))],
        compiler_params=pltpu.CompilerParams(vmem_limit_bytes=MIB),
        cost_estimate=pl.CostEstimate(flops=0, bytes_accessed=4 * size, transcendentals=0),
    )(gate_w, up_w, after)


def expert_kernel(early, late_steps, down_steps, *refs):
    near, far, gate_w, up_w, down_w = refs[:5]
    loaded = refs[5 : 5 + 2 * early]
    keep, send, lead, gate_v, up_v, down_v, gate_acc, up_acc, out_acc, sems = refs[5 + 2 * early :]
    half = near.shape[0]
    width = keep.shape[1]
    rep = lax.axis_index("rep")
    expert = lax.axis_index("exp") * gate_w.shape[0] + rep
    late_rows, hidden_width = gate_v.shape
    late_first = width - late_rows
    step_rows, down_rows = late_rows // late_steps, hidden_width // down_steps

    late, down = [], []
    for k in range(late_steps):
        there, here = pl.ds(late_first + k * step_rows, step_rows), pl.ds(k * step_rows, step_rows)
        late.append(
            (
                pltpu.make_async_copy(gate_w.at[rep, there], gate_v.at[here], sems.at[2 * k]),
                pltpu.make_async_copy(up_w.at[rep, there], up_v.at[here], sems.at[2 * k + 1]),
            )
        )
    for k in range(down_steps):
        rows = pl.ds(k * down_rows, down_rows)
        down.append(
            pltpu.make_async_copy(down_w.at[rep, rows], down_v.at[rows], sems.at[2 * late_steps + k])
        )
    for pair in late:
        for copy in pair:
            copy.start()
    for copy in down:
        copy.start()
    lead_cols = pl.ds(0, lead.shape[1])
    last = 2 * late_steps + down_steps
    leads = [
        pltpu.make_async_copy(near.at[:, lead_cols], lead.at[pl.ds(0, half)], sems.at[last]),
        pltpu.make_async_copy(far.at[:, lead_cols], lead.at[pl.ds(half, half)], sems.at[last + 1]),
    ]
    for copy in leads:
        copy.start()
    for copy in leads:
        copy.wait()

    def tokens(first, rows):
        if first == 0:
            return lead[...]
        cols = slice(first, first + rows)
        return jnp.concatenate([near[:, cols], far[:, cols]], axis=0)

    first = 0
    for k in range(early):
        gate_p, up_p = loaded[2 * k], loaded[2 * k + 1]
        x = tokens(first, gate_p.shape[0])
        gate = jnp.dot(x, gate_p[...], preferred_element_type=jnp.float32)
        gate_acc[...] = gate if k == 0 else gate_acc[...] + gate
        upper = jnp.dot(x, up_p[...], preferred_element_type=jnp.float32)
        up_acc[...] = upper if k == 0 else up_acc[...] + upper
        first += gate_p.shape[0]
    for k, (gate_copy, up_copy) in enumerate(late):
        here = slice(k * step_rows, (k + 1) * step_rows)
        x = tokens(first, step_rows)
        gate_copy.wait()
        gate_acc[...] += jnp.dot(x, gate_v[here, :], preferred_element_type=jnp.float32)
        up_copy.wait()
        up_acc[...] += jnp.dot(x, up_v[here, :], preferred_element_type=jnp.float32)
        first += step_rows
    gate = gate_acc[...]
    hidden = (gate / (1.0 + jnp.exp(-gate)) * up_acc[...]).astype(jnp.bfloat16)
    for k, copy in enumerate(down):
        cols = slice(k * down_rows, (k + 1) * down_rows)
        copy.wait()
        term = jnp.dot(hidden[:, cols], down_v[cols, :], preferred_element_type=jnp.float32)
        out_acc[...] = term if k == 0 else out_acc[...] + term
    chosen = lax.broadcasted_iota(jnp.int32, (half, LANES), 1) == expert
    for rows, piece, out in ((slice(half, 2 * half), far, send), (slice(0, half), near, keep)):
        tail = piece[:, width:].astype(jnp.float32)
        weight = jnp.sum(jnp.where(chosen, tail, 0.0), axis=1, keepdims=True)
        out[...] = (weight * out_acc[rows, :]).astype(out.dtype)


def run_experts(near, far, loaded, gate_w, up_w, down_w):
    half = near.shape[0]
    _, width, hidden = gate_w.shape
    padded = -(-hidden // LANES) * LANES
    late_rows = width - sum(gate_p.shape[0] for gate_p, _ in loaded)
    late_steps = 2
    down_steps = hidden // 256 if hidden % 256 == 0 else 1
    lead_rows = loaded[0][0].shape[0]
    scratch = 4 * half * lead_rows + 4 * late_rows * padded + 2 * hidden * width + 8 * half * (2 * padded + width)
    return pl.pallas_call(
        functools.partial(expert_kernel, len(loaded), late_steps, down_steps),
        out_shape=(
            jax.ShapeDtypeStruct((half, width), jnp.float32),
            jax.ShapeDtypeStruct((half, width), jnp.bfloat16),
        ),
        in_specs=[VMEM, VMEM, HBM, HBM, HBM] + [VMEM] * (2 * len(loaded)),
        out_specs=(VMEM, VMEM),
        scratch_shapes=[
            pltpu.VMEM((2 * half, lead_rows), jnp.bfloat16),
            pltpu.VMEM((late_rows, hidden), jnp.bfloat16),
            pltpu.VMEM((late_rows, hidden), jnp.bfloat16),
            pltpu.VMEM((hidden, width), jnp.bfloat16),
            pltpu.VMEM((2 * half, hidden), jnp.float32),
            pltpu.VMEM((2 * half, hidden), jnp.float32),
            pltpu.VMEM((2 * half, width), jnp.float32),
            pltpu.SemaphoreType.DMA((2 * late_steps + down_steps + 2,)),
        ],
        compiler_params=pltpu.CompilerParams(vmem_limit_bytes=scratch + 4 * MIB),
    )(near, far, gate_w, up_w, down_w, *(ref for pair in loaded for ref in pair))


def body(mesh_shape, tokens, expert_ids, gate_ints, gate_weight, up_weight, down_weight):
    width = tokens.shape[1]
    assert gate_weight.shape[0] == mesh_shape[0]
    gate_weight, up_weight, down_weight = (
        pltpu.with_memory_space_constraint(w, pltpu.HBM)
        for w in (gate_weight, up_weight, down_weight)
    )

    def swap(x, exp_xor, offsets):
        return lax.ppermute(x, AXES, partner(mesh_shape, exp_xor, offsets))

    stay = ((0, 0), (0, 0))

    gathered = pack(tokens, expert_ids, gate_ints)
    rounds = exchange_rounds(mesh_shape)
    shares = [e * width // 16 for e in EARLY_SHARES]
    loaded, first = [], 0

    def load(rows):
        nonlocal first
        loaded.append(load_early(gate_weight, up_weight, gathered, first, rows))
        first += rows

    for at, offsets in enumerate(rounds):
        if at < len(shares) - 1:
            load(shares[at])
        gathered = jnp.concatenate(
            [gathered] + [swap(gathered, 0, offset) for offset in offsets], axis=0
        )
        if at < len(shares) - 1:
            gathered, loaded[-1] = lax.optimization_barrier((gathered, loaded[-1]))
    load(shares[-1])
    far = swap(gathered, 1, stay)
    keep, send = run_experts(gathered, far, loaded, gate_weight, up_weight, down_weight)
    total = keep + swap(send, 1, stay).astype(jnp.float32)
    for offsets in reversed(rounds):
        part = total.shape[0] // (len(offsets) + 1)
        pieces = [total[i * part : (i + 1) * part] for i in range(len(offsets) + 1)]
        total = pieces[0]
        moves = list(zip(pieces[1:], offsets))
        for piece, offset in moves if offsets is rounds[-1] else reversed(moves):
            total = total + swap(piece.astype(jnp.bfloat16), 0, offset).astype(jnp.float32)
    return total.astype(jnp.bfloat16)


def solution(mesh):
    mesh_shape = tuple(mesh.shape[a] for a in AXES)
    return jax.shard_map(
        functools.partial(body, mesh_shape),
        mesh=mesh,
        in_specs=(
            P(AXES, None),
            P(AXES, None),
            P(AXES, None),
            P("exp", None, "tp"),
            P("exp", None, "tp"),
            P("exp", "tp", None),
        ),
        out_specs=P(AXES, None),
        check_vma=False,
    )
```
